32 devices in a mesh: az: 4 (over z), rg: 8 (over y, x, core).
Axes of the slice: x: 2, y: 2, z: 4, core: 2. Of those that a mesh axis runs over, the one named last changes fastest.
Arguments:
- echo_planes: float32 [2, 4096, 8192], P(None, 'rg', 'az'), may hold values from -6 to 6
- pulse_phase: float32 [384], replicated, may hold values from -3.140625 to 3.140625
- band_offsets: int32 [4, 4, 8], P(None, 'az', 'rg'), may hold values from 0 to 57, as said below
- band_weights: float32 [4, 4, 8, 4096], P(None, 'az', None, 'rg'), may hold values from -2 to 2
- azimuth_rate: float32 [4096], P('rg'), may hold values from 16 to 256
Outputs:
- focused: float32 [2, 4096, 8192], P(None, 'rg', 'az')
The draws below stay inside these ranges and needn't reach their ends.
Inputs may be any that keep to these rules, and one draw needn't show every extreme that they name: band_offsets[b, j, r] counts rows from a bin's own row; the value 57 occurs in every draw.
All inputs are finite; a program needn't handle non-finite values.
Results may differ from the reference program's by a relative error of at most 0.004.
Values may be sent and summed in bfloat16 or wider, within the bound.
A program may use at most 192 MiB of HBM per device.

```python
import math
import jax
import jax.numpy as jnp
from jax import lax

PULSES = 8192
RANGE_DEV = 512
CODE_LEN = 384
TAPS = 8
MAX_SHIFT = 57
BANKS = 4
BLOCKS = 8
PULSE_DEV = 2048
GROUP_BINS = 512
RANGE = 4096
RIM_ROWS = 64


def draw_band_offsets(key, part):
    first_key = jax.random.fold_in(key, 11)
    second_key = jax.random.fold_in(key, 23)
    total_count = BANKS * BANKS * BLOCKS
    values = jax.random.randint(first_key, (total_count,), 0, MAX_SHIFT + 1)
    chosen = jax.random.randint(second_key, (), 0, total_count)
    flattened = jnp.where(jnp.arange(total_count) == chosen, MAX_SHIFT, values)
    return flattened.reshape(BANKS, BANKS, BLOCKS).astype(jnp.int32)


def level_of(key, dims, pieces, low, high):
    gain, own = 1.0, jax.random.fold_in(key, 6)
    for axis_at, blocks in pieces:
        heights = jnp.exp(jax.random.uniform(jax.random.fold_in(own, axis_at), (blocks,), jnp.float32, low / len(pieces), high / len(pieces)))
        gain = gain * jnp.repeat(heights, dims[axis_at] // blocks).reshape([-1 if axis == axis_at else 1 for axis in range(len(dims))])
    return gain


def centred(key, dims, scale, bound, shards=(), kind=jnp.bfloat16):
    entries = scale * jax.random.normal(key, dims, jnp.float32)
    if shards:
        entries = entries * level_of(key, dims, shards, -0.22, 0.18)
    return jnp.clip(entries, -bound, bound).astype(kind)


def setup_inputs(seed: int = 0) -> dict:
    seeds = jax.random.split(jax.random.key(seed), 6)
    echo_planes = centred(seeds[0], (2, RANGE, PULSES), 1.0, 6.0, ((1, 8), (2, 4)), jnp.float32)
    pulse_phase = jnp.clip(jax.random.uniform(seeds[1], (CODE_LEN,), jnp.float32, -3.140625, 3.140625), -3.140625, 3.140625)
    band_offsets = draw_band_offsets(jax.random.fold_in(seeds[5], 71), 0)
    band_weights = centred(seeds[3], (BANKS, BANKS, TAPS, RANGE), TAPS ** -0.5, 2.0, ((1, 4), (3, 8)), jnp.float32)
    azimuth_rate = jnp.clip(jnp.exp(math.log(256.0) - 2.7725887 * jax.random.uniform(seeds[4], (RANGE,), jnp.float32) ** level_of(seeds[4], (RANGE,), ((0, 8),), -0.2, 0.2)), 16.0, 256.0)
    return {"echo_planes": echo_planes, "pulse_phase": pulse_phase, "band_offsets": band_offsets, "band_weights": band_weights, "azimuth_rate": azimuth_rate}


def angle_pair(product, period):
    angles = 2.0 * math.pi / period * (product % period).astype(jnp.float32)
    return (jnp.cos(angles), jnp.sin(angles))

def pick_rows(source, indices):
    return source[indices]

def reference(echo_planes, pulse_phase, band_offsets, band_weights, azimuth_rate):
    waveform = lax.complex(jnp.cos(pulse_phase), jnp.sin(pulse_phase))
    fft_length = 2 * RANGE
    wave_hat = jnp.conj(jnp.fft.fft(waveform, n=fft_length))
    bin_index = jnp.arange(PULSE_DEV, dtype=jnp.int32)
    banks_first = echo_planes.reshape(2, RANGE, BANKS, PULSE_DEV).transpose(2, 0, 1, 3)

    def per_bank(packed):
        planes, bank_index = packed
        echo_block = lax.complex(planes[0], planes[1])
        compressed = jnp.fft.ifft(jnp.fft.fft(echo_block, n=fft_length, axis=0) * wave_hat[:, None], axis=0)[:RANGE]
        compressed = compressed / math.sqrt(CODE_LEN)
        spectrum = jnp.fft.fft(compressed, axis=1)
        cos_part, sin_part = angle_pair(bank_index * bin_index, PULSES)
        spectrum = spectrum * lax.complex(cos_part, -sin_part)[None, :]
        real_part = lax.optimization_barrier(spectrum.real.astype(jnp.bfloat16)).astype(jnp.float32)
        imag_part = lax.optimization_barrier(spectrum.imag.astype(jnp.bfloat16)).astype(jnp.float32)
        return jnp.stack([real_part, imag_part])
    partial_value = lax.map(per_bank, (banks_first, jnp.arange(BANKS, dtype=jnp.int32)))
    spectrum = jnp.fft.fft(lax.complex(partial_value[:, 0], partial_value[:, 1]), axis=0)

    def per_group(packed):
        spectrum_bank, offsets_bank, weights_bank, bank_index = packed
        group_data = spectrum_bank.reshape(RANGE, BANKS, GROUP_BINS).transpose(1, 0, 2)
        padded = jnp.concatenate([group_data, jnp.zeros((BANKS, RIM_ROWS, GROUP_BINS), group_data.dtype)], axis=1)
        start_rows = jnp.arange(RANGE, dtype=jnp.int32)[None, :] + jnp.repeat(offsets_bank, RANGE_DEV, axis=1)
        migrated = jnp.zeros_like(group_data)
        for tap_index in range(TAPS):
            selected = jax.vmap(pick_rows)(padded, start_rows + tap_index)
            migrated = migrated + weights_bank[:, tap_index, :, None] * selected
        doppler_bin = jnp.arange(PULSE_DEV, dtype=jnp.int32).reshape(BANKS, GROUP_BINS) + PULSE_DEV * bank_index
        centered = jnp.where(doppler_bin < PULSES // 2, doppler_bin, doppler_bin - PULSES)
        doppler_freq = centered.astype(jnp.float32) / PULSES
        base_phase = jnp.pi * doppler_freq * doppler_freq
        phases = base_phase[:, None, :] * azimuth_rate[None, :, None]
        filtered = migrated * lax.complex(jnp.cos(phases), jnp.sin(phases))
        return filtered.transpose(1, 0, 2).reshape(RANGE, PULSE_DEV)
    filtered = lax.map(per_group, (spectrum, band_offsets, band_weights, jnp.arange(BANKS, dtype=jnp.int32)))
    folded = jnp.fft.ifft(filtered, axis=0)
    bank_ids = jnp.arange(BANKS, dtype=jnp.int32)
    cos_part, sin_part = angle_pair(bank_ids[:, None] * bin_index[None, :], PULSES)
    folded = folded * lax.complex(cos_part, sin_part)[:, None, :]
    real_part = lax.optimization_barrier(folded.real.astype(jnp.bfloat16)).astype(jnp.float32)
    imag_part = lax.optimization_barrier(folded.imag.astype(jnp.bfloat16)).astype(jnp.float32)
    focused_image = jnp.fft.ifft(lax.complex(real_part, imag_part), axis=2)
    planes = jnp.stack([focused_image.real, focused_image.imag]).astype(jnp.float32)
    return planes.transpose(0, 2, 1, 3).reshape(2, RANGE, PULSES)
```

```python
import functools
import math

import jax
import jax.numpy as jnp
import ml_dtypes
import numpy as np
from jax import lax
from jax.experimental import pallas as pl
from jax.experimental.pallas import tpu as pltpu
from jax.sharding import PartitionSpec as P

RIM_ROWS = 64
TILE = 128
HALF = 64
CALL_ROWS = 128
VMEM_LIMIT = 56 * 1024 * 1024
bf16 = jnp.bfloat16
f32 = jnp.float32


def passed_along(value, axis, steps):
    count = lax.axis_size(axis)
    initial, last = (max(0, -steps), min(count, count - steps))
    return lax.ppermute(value, axis, [(source, source + steps) for source in range(initial, last)])


def butterfly(values, sign, turn):
    count = len(values)
    if count == 1:
        return values
    even = butterfly(values[0::2], sign, turn)
    odd = butterfly(values[1::2], sign, turn)
    lower, upper = [], []
    for k in range(count // 2):
        if k == 0:
            turned = odd[k]
        elif 4 * k == count:
            turned = turn(odd[k], 0.0, float(sign))
        else:
            angle = sign * 2.0 * math.pi * k / count
            turned = turn(odd[k], math.cos(angle), math.sin(angle))
        lower.append(jax.tree.map(lambda x, y: x + y, even[k], turned))
        upper.append(jax.tree.map(lambda x, y: x - y, even[k], turned))
    return lower + upper


def turn_pair(value, c, s):
    re, im = value
    if c == 0.0:
        return (-im, re) if s > 0 else (im, -re)
    return (re * c - im * s, im * c + re * s)


def split(value):
    high = value.astype(bf16)
    return high, (value - high.astype(f32)).astype(bf16)


def forward_kernel(tiles, blocks, first, second, banks, *refs):
    code_ref = refs[0]
    block_refs = refs[1 : 1 + blocks]
    twist_ref, high_ref, low_ref, out_ref, band, window, comp, spread_high, spread_low = refs[1 + blocks :]
    step = pl.program_id(0)
    rows = tiles * TILE
    span = code_ref.shape[2]

    @pl.when(step == 0)
    def _():
        def shifted(index):
            wide = jnp.broadcast_to(code_ref[index], (TILE, span))
            return split(pltpu.roll(wide, 0, 1, stride=1, stride_axis=0))

        for part, (c, s) in enumerate(zip(shifted(0), shifted(1))):
            at = 2 * TILE * part
            band[at : at + TILE, :span] = c
            band[at : at + TILE, span:] = s
            band[at + TILE : at + 2 * TILE, :span] = -s
            band[at + TILE : at + 2 * TILE, span:] = c

    for index, block_ref in enumerate(block_refs):
        window[:, index * TILE : (index + 1) * TILE, :] = block_ref[...].astype(bf16)
    for tile in range(tiles):
        at = tile * TILE
        both = jnp.concatenate([window[0, at : at + span], window[1, at : at + span]], axis=0)
        product = jnp.dot(band[...], both, preferred_element_type=f32)
        comp[step, 0, at : at + TILE] = product[:TILE] + product[2 * TILE : 3 * TILE]
        comp[step, 1, at : at + TILE] = product[TILE : 2 * TILE] + product[3 * TILE :]

    @pl.when(step == first - 1)
    def _():
        @pl.loop(0, rows // 16)
        def _(chunk):
            at = pl.multiple_of(chunk * 16, 16)
            for lane in range(0, second, 128):
                lanes = slice(lane, lane + 128)
                values = [(comp[a, 0, pl.ds(at, 16), lanes], comp[a, 1, pl.ds(at, 16), lanes]) for a in range(first)]
                values = butterfly(values, -1, turn_pair)
                for k, (re, im) in enumerate(values):
                    c, s = twist_ref[0, k : k + 1, lanes], twist_ref[1, k : k + 1, lanes]
                    where = pl.ds(pl.multiple_of(k * rows + at, 16), 16)
                    for base, value in ((0, re * c + im * s), (second, im * c - re * s)):
                        high, low = split(value)
                        spread_high[where, base + lane : base + lane + 128] = high
                        spread_low[where, base + lane : base + lane + 128] = low

        high = spread_high[...]
        result = (
            jnp.dot(high, high_ref[...], preferred_element_type=f32)
            + jnp.dot(high, low_ref[...], preferred_element_type=f32)
            + jnp.dot(spread_low[...], high_ref[...], preferred_element_type=f32)
        )
        for k in range(first):
            for g in range(banks):
                out_ref[g, :, k * 128 : (k + 1) * 128] = result[
                    k * rows : (k + 1) * rows, g * 128 : (g + 1) * 128
                ].astype(bf16)


def forward_call(code, echo, rims, start, rows, twist, high, low, banks):
    first, second = twist.shape[1:]
    span = code.shape[2]
    tiles = rows // TILE
    blocks = tiles + span // TILE - 1
    own = echo.shape[1] // TILE
    operands, specs = [], []
    for index in range(blocks):
        place = start // TILE + index
        if place < own:
            operands.append(echo)
            specs.append(pl.BlockSpec((2, TILE, second), functools.partial(lambda p, s: (0, p, s), place)))
        else:
            operands.append(rims[place - own])
            specs.append(pl.BlockSpec((2, TILE, second), lambda s: (0, 0, s)))
    whole = lambda shape: pl.BlockSpec(shape, lambda s: (0,) * len(shape))
    return pl.pallas_call(
        functools.partial(forward_kernel, tiles, blocks, first, second, banks),
        grid=(first,),
        in_specs=[whole(code.shape)] + specs + [whole(twist.shape), whole(high.shape), whole(low.shape)],
        out_specs=whole((banks, rows, first * 128)),
        out_shape=jax.ShapeDtypeStruct((banks, rows, first * 128), bf16),
        scratch_shapes=[
            pltpu.VMEM((4 * TILE, 2 * span), bf16),
            pltpu.VMEM((2, blocks * TILE, second), bf16),
            pltpu.VMEM((first, 2, rows, second), f32),
            pltpu.VMEM((first * rows, 2 * second), bf16),
            pltpu.VMEM((first * rows, 2 * second), bf16),
        ],
        compiler_params=pltpu.CompilerParams(vmem_limit_bytes=VMEM_LIMIT),
        cost_estimate=pl.CostEstimate(flops=rows * 24_000_000, bytes_accessed=rows * 30_000, transcendentals=0),
        name="forward",
    )(code, *operands, twist, high, low)


SINE = [(-1) ** n * (2.0 * math.pi) ** (2 * n + 1) / math.factorial(2 * n + 1) for n in range(6)]


def cosine_turns(turns):
    rest = turns - jnp.round(turns)
    u = 0.25 - jnp.abs(rest)
    z = u * u
    total = jnp.full_like(z, SINE[-1])
    for factor in reversed(SINE[:-1]):
        total = total * z + factor
    return total * u


def migrate_kernel(tiles, banks, taps, width, offset_ref, weight_ref, rate_ref, base_ref, own_ref, next_ref, out_ref, band, spec_high, spec_low, moved):
    rows = tiles * TILE
    span = TILE + RIM_ROWS

    @pl.when(pl.program_id(0) == 0)
    def _():
        for b in range(banks):
            steps = lax.broadcasted_iota(jnp.int32, (TILE, span), 1) - lax.broadcasted_iota(jnp.int32, (TILE, span), 0) - offset_ref[b]
            for tile in range(tiles):
                total = jnp.zeros((TILE, span), f32)
                for t in range(taps):
                    total = jnp.where(steps == t, weight_ref[b, tile * TILE : (tile + 1) * TILE, t : t + 1], total)
                high, low = split(total)
                band[b, tile, :TILE] = high
                band[b, tile, TILE:] = low

    lane_id = lax.broadcasted_iota(jnp.int32, (1, 128), 1)
    left = lane_id < HALF
    minus = jnp.where(left, -1.0, 1.0).astype(f32)

    def turn_lanes(value, c, s):
        crossed = pltpu.roll(value, HALF, 1) * minus
        if c == 0.0:
            return crossed if s > 0 else -crossed
        return value * c + crossed * s

    def combine(ref, at, place):
        for lane in range(0, width, 128):
            lanes = slice(lane, lane + 128)
            values = butterfly([ref[a, pl.ds(at, 32), lanes].astype(f32) for a in range(banks)], -1, turn_lanes)
            for b, value in enumerate(values):
                high, low = split(value)
                spec_high[b, pl.ds(place, 32), lanes] = high
                spec_low[b, pl.ds(place, 32), lanes] = low

    @pl.loop(0, rows // 32)
    def _(chunk):
        at = pl.multiple_of(chunk * 32, 32)
        combine(own_ref, at, at)

    for at in range(0, RIM_ROWS, 32):
        combine(next_ref, at, rows + at)

    for b in range(banks):
        for tile in range(tiles):
            at = tile * TILE
            product = jnp.dot(band[b, tile], spec_high[b, at : at + span], preferred_element_type=f32)
            rest = jnp.dot(band[b, tile, :TILE], spec_low[b, at : at + span], preferred_element_type=f32)
            moved[b, at : at + TILE] = product[:TILE] + product[TILE:] + rest

    quarter = jnp.where(left, 0.0, 0.25).astype(f32)

    @pl.loop(0, rows // 32)
    def _(chunk):
        at = pl.ds(pl.multiple_of(chunk * 32, 32), 32)
        rate = rate_ref[at]
        for lane in range(0, width, 128):
            lanes = slice(lane, lane + 128)
            values = []
            for b in range(banks):
                wave = cosine_turns(rate * base_ref[b : b + 1, lanes] - quarter)
                crossed = pltpu.roll(wave, HALF, 1)
                value = moved[b, at, lanes]
                values.append(
                    value * jnp.where(left, wave, crossed)
                    + pltpu.roll(value, HALF, 1) * jnp.where(left, -crossed, wave)
                )
            for a, value in enumerate(butterfly(values, 1, turn_lanes)):
                out_ref[a, at, lanes] = value.astype(bf16)


def migrate_call(offsets, weights, rate, base, own, following, start):
    banks, rows, lanes = own.shape
    taps = weights.shape[2]
    width = min(256, lanes)
    tiles = rows // TILE
    return pl.pallas_call(
        functools.partial(migrate_kernel, tiles, banks, taps, width),
        grid=(lanes // width,),
        in_specs=[
            pl.BlockSpec(memory_space=pltpu.SMEM),
            pl.BlockSpec((banks, rows, taps), lambda s: (0, start // rows, 0)),
            pl.BlockSpec((rows, 128), lambda s: (start // rows, 0)),
            pl.BlockSpec((banks, width), lambda s: (0, s)),
            pl.BlockSpec((banks, rows, width), lambda s: (0, 0, s)),
            pl.BlockSpec((banks, RIM_ROWS, width), lambda s: (0, 0, s)),
        ],
        out_specs=pl.BlockSpec((banks, rows, width), lambda s: (0, 0, s)),
        out_shape=jax.ShapeDtypeStruct(own.shape, bf16),
        scratch_shapes=[
            pltpu.VMEM((banks, tiles, 2 * TILE, TILE + RIM_ROWS), bf16),
            pltpu.VMEM((banks, rows + RIM_ROWS, width), bf16),
            pltpu.VMEM((banks, rows + RIM_ROWS, width), bf16),
            pltpu.VMEM((banks, rows, width), f32),
        ],
        compiler_params=pltpu.CompilerParams(vmem_limit_bytes=VMEM_LIMIT),
        cost_estimate=pl.CostEstimate(flops=rows * 10_000_000, bytes_accessed=rows * 30_000, transcendentals=0),
        name="migrate",
    )(offsets, weights, rate, base, own, following)


def inverse_kernel(first, second, banks, in_ref, twist_ref, high_ref, low_ref, *refs):
    out_ref, gathered, turned = refs[-3:]
    for k in range(first):
        for g in range(banks):
            gathered[k * TILE : (k + 1) * TILE, g * 128 : (g + 1) * 128] = in_ref[g, :, k * 128 : (k + 1) * 128]
    value = gathered[...]
    across = (((1,), (1,)), ((), ()))
    turned[...] = lax.dot_general(value, high_ref[...], across, preferred_element_type=f32) + lax.dot_general(
        value, low_ref[...], across, preferred_element_type=f32
    )

    @pl.loop(0, TILE // 16)
    def _(chunk):
        at = pl.multiple_of(chunk * 16, 16)
        for lane in range(0, second, 128):
            values = []
            for k in range(first):
                where = pl.ds(pl.multiple_of(k * TILE + at, 16), 16)
                re = turned[where, lane : lane + 128]
                im = turned[where, second + lane : second + lane + 128]
                c = twist_ref[0, k : k + 1, lane : lane + 128]
                s = twist_ref[1, k : k + 1, lane : lane + 128]
                values.append((re * c - im * s, im * c + re * s))
            for a, (re, im) in enumerate(butterfly(values, 1, turn_pair)):
                lanes = slice(a * second + lane, a * second + lane + 128)
                out_ref[0, pl.ds(at, 16), lanes] = re
                out_ref[1, pl.ds(at, 16), lanes] = im


def inverse_call(previous, received, twist, high, low, start, total_rows):
    banks, rows, lanes = received.shape
    first, second = twist.shape[1:]
    whole = lambda shape: pl.BlockSpec(shape, lambda s: (0,) * len(shape))
    specs = [pl.BlockSpec((banks, TILE, lanes), lambda s: (0, s, 0)), whole(twist.shape), whole(high.shape), whole(low.shape)]
    operands = [received, twist, high, low]
    aliases = {}
    if previous is not None:
        specs.append(pl.BlockSpec(memory_space=pl.ANY))
        operands.append(previous)
        aliases = {4: 0}
    return pl.pallas_call(
        functools.partial(inverse_kernel, first, second, banks),
        grid=(rows // TILE,),
        in_specs=specs,
        out_specs=pl.BlockSpec((2, TILE, first * second), lambda s: (0, start // TILE + s, 0)),
        out_shape=jax.ShapeDtypeStruct((2, total_rows, first * second), f32),
        scratch_shapes=[
            pltpu.VMEM((first * TILE, 2 * second), bf16),
            pltpu.VMEM((first * TILE, 2 * second), f32),
        ],
        input_output_aliases=aliases,
        compiler_params=pltpu.CompilerParams(vmem_limit_bytes=VMEM_LIMIT),
        cost_estimate=pl.CostEstimate(flops=rows * 10_000_000, bytes_accessed=rows * 30_000, transcendentals=0),
        name="inverse",
    )(*operands)


def tables(banks, first, second):
    pulses = banks * first * second
    inner = np.arange(second)
    highs, lows, twists = [], [], []
    for bank in range(banks):
        steps = banks * inner + bank
        angle = 2.0 * np.pi * ((steps[:, None] * inner[None, :]) % (banks * second)) / (banks * second)
        c, s = np.cos(angle), np.sin(angle)
        re_out = np.concatenate([c, s], axis=0).reshape(2 * second, banks, HALF)
        im_out = np.concatenate([-s, c], axis=0).reshape(2 * second, banks, HALF)
        table = np.stack([re_out, im_out], axis=2).reshape(2 * second, 2 * second)
        high = table.astype(ml_dtypes.bfloat16)
        highs.append(high)
        lows.append((table - high.astype(np.float64)).astype(ml_dtypes.bfloat16))
        angle = 2.0 * np.pi * ((np.arange(first)[:, None] * steps[None, :]) % pulses) / pulses
        twists.append(np.stack([np.cos(angle), np.sin(angle)]).astype(np.float32))
    return np.stack(highs), np.stack(lows), np.stack(twists)


def local(echo_planes, pulse_phase, band_offsets, band_weights, azimuth_rate):
    banks = lax.axis_size("az")
    bank = lax.axis_index("az")
    row_count, pulse_local = echo_planes.shape[1:]
    pulse_count = pulse_local * banks
    second = HALF * banks
    first = pulse_local // second
    code_length = pulse_phase.shape[0]
    reach = -(-code_length // TILE)
    rims = [
        passed_along(echo_planes[:, i * TILE : (i + 1) * TILE].astype(bf16), "rg", -1) for i in range(reach)
    ]
    highs, lows, twists = tables(banks, first, second)
    pick = lambda stack: lax.dynamic_index_in_dim(jnp.asarray(stack), bank, 0, keepdims=False)
    high, low, twist = pick(highs), pick(lows), pick(twists)
    span = (reach + 1) * TILE
    norm_scale = 1.0 / math.sqrt(code_length)
    code = jnp.stack([jnp.cos(pulse_phase), jnp.sin(pulse_phase)]) * norm_scale
    code = jnp.pad(code, ((0, 0), (0, span - code_length)))[:, None, :]

    offsets = band_offsets[:, 0, 0]
    weights = band_weights[:, 0].transpose(0, 2, 1)
    rate = jnp.broadcast_to(azimuth_rate[:, None], (row_count, 128))
    lane = jnp.arange(first * 128, dtype=jnp.int32)
    bins = bank * (HALF * first) + first * (lane % HALF) + lane // 128
    bins = bins[None, :] + pulse_local * jnp.arange(banks, dtype=jnp.int32)[:, None]
    centered = jnp.where(bins < pulse_count // 2, bins, bins - pulse_count)
    frequency = centered.astype(f32) / pulse_count
    base = 0.5 * frequency * frequency

    starts = list(range(0, row_count, CALL_ROWS))
    swap = lambda value: lax.all_to_all(value, "az", split_axis=0, concat_axis=0, tiled=True)
    spectra = [swap(forward_call(code, echo_planes, rims, s, CALL_ROWS, twist, high, low, banks)) for s in starts]
    spectra.append(passed_along(spectra[0][:, :RIM_ROWS], "rg", -1))
    folded = [
        swap(migrate_call(offsets, weights, rate, base, spectra[i], spectra[i + 1], s)) for i, s in enumerate(starts)
    ]
    twist = twist * (1.0 / pulse_count)
    out = None
    for s, value in zip(starts, folded):
        out = inverse_call(out, value, twist, high, low, s, row_count)
    return out


def solution(mesh):
    in_specs = (P(None, "rg", "az"), P(), P(None, "az", "rg"), P(None, "az", None, "rg"), P("rg"))
    out_specs = P(None, "rg", "az")
    return jax.shard_map(local, mesh=mesh, in_specs=in_specs, out_specs=out_specs, check_vma=False)
```

```python
import functools
import math

import jax
import jax.numpy as jnp
import ml_dtypes
import numpy as np
from jax import lax
from jax.experimental import pallas as pl
from jax.experimental.pallas import tpu as pltpu
from jax.sharding import PartitionSpec as P

RIM_ROWS = 64
TILE = 128
HALF = 64
VMEM_LIMIT = 56 * 1024 * 1024
bf16 = jnp.bfloat16
f32 = jnp.float32


def butterfly(values, sign, turn):
    count = len(values)
    if count == 1:
        return values
    even = butterfly(values[0::2], sign, turn)
    odd = butterfly(values[1::2], sign, turn)
    lower, upper = [], []
    for k in range(count // 2):
        if k == 0:
            turned = odd[k]
        elif 4 * k == count:
            turned = turn(odd[k], 0.0, float(sign))
        else:
            angle = sign * 2.0 * math.pi * k / count
            turned = turn(odd[k], math.cos(angle), math.sin(angle))
        lower.append(jax.tree.map(lambda x, y: x + y, even[k], turned))
        upper.append(jax.tree.map(lambda x, y: x - y, even[k], turned))
    return lower + upper


def turn_pair(value, c, s):
    re, im = value
    if c == 0.0:
        return (-im, re) if s > 0 else (im, -re)
    return (re * c - im * s, im * c + re * s)


def split(value):
    high = value.astype(bf16)
    return high, (value - high.astype(f32)).astype(bf16)


SINE = [(-1) ** n * (2.0 * math.pi) ** (2 * n + 1) / math.factorial(2 * n + 1) for n in range(6)]


def cosine_turns(turns):
    rest = turns - jnp.round(turns)
    u = 0.25 - jnp.abs(rest)
    z = u * u
    total = jnp.full_like(z, SINE[-1])
    for factor in reversed(SINE[:-1]):
        total = total * z + factor
    return total * u


def focus_kernel(
    banks, first, second, taps, echo_ref, code_ref, twist_ref, high_ref, low_ref, offset_ref, weight_ref, rate_ref, base_ref, out_ref,
    stage, window, band, comp, spread_high, spread_low, result, send, spectra, taps_band, spec_high, spec_low, moved, folded,
    load_sem, rim_send, rim_recv, out_send, out_recv, edge_send, edge_recv, back_send, back_recv, own_sem,
):
    bank, block = lax.axis_index("az"), lax.axis_index("rg")
    block_count = lax.axis_size("rg")
    rows = echo_ref.shape[1]
    chunks = rows // TILE
    span = code_ref.shape[2]
    reach = span // TILE - 1
    width = min(256, first * 128)
    wide = TILE + RIM_ROWS
    has_next = block < block_count - 1
    has_previous = block > 0

    def load(chunk):
        at = slice(chunk * TILE, (chunk + 1) * TILE)
        return pltpu.make_async_copy(echo_ref.at[:, at], stage.at[:, at], load_sem.at[chunk])

    def rim(piece):
        return pltpu.make_async_remote_copy(
            src_ref=window.at[:, pl.ds(piece * TILE, TILE)],
            dst_ref=window.at[:, pl.ds(rows + piece * TILE, TILE)],
            send_sem=rim_send.at[piece],
            recv_sem=rim_recv.at[piece],
            device_id={"rg": lax.rem(block + block_count - 1, block_count)},
            device_id_type=pl.DeviceIdType.MESH,
        )

    def edge():
        return pltpu.make_async_remote_copy(
            src_ref=spectra.at[:, pl.ds(0, RIM_ROWS)],
            dst_ref=spectra.at[:, pl.ds(rows, RIM_ROWS)],
            send_sem=edge_send,
            recv_sem=edge_recv,
            device_id={"rg": lax.rem(block + block_count - 1, block_count)},
            device_id_type=pl.DeviceIdType.MESH,
        )

    def exchange(source, target, send_sem, recv_sem, chunk, distance):
        peer = lax.rem(bank + distance, banks)
        return pltpu.make_async_remote_copy(
            src_ref=source.at[peer, pl.ds(pl.multiple_of(chunk * TILE, TILE), TILE)],
            dst_ref=target.at[bank, pl.ds(pl.multiple_of(chunk * TILE, TILE), TILE)],
            send_sem=send_sem.at[chunk, distance - 1],
            recv_sem=recv_sem.at[chunk, distance - 1],
            device_id={"az": peer},
            device_id_type=pl.DeviceIdType.MESH,
        )

    outward = functools.partial(exchange, send, spectra, out_send, out_recv)
    backward = functools.partial(exchange, folded, out_ref, back_send, back_recv)

    def own_back(chunk):
        at = pl.ds(pl.multiple_of(chunk * TILE, TILE), TILE)
        return pltpu.make_async_copy(folded.at[bank, at], out_ref.at[bank, at], own_sem.at[chunk])

    for chunk in range(chunks):
        load(chunk).start()

    barrier = pltpu.get_barrier_semaphore()
    for distance in range(1, banks):
        pl.semaphore_signal(
            barrier, inc=1, device_id={"az": lax.rem(bank + distance, banks)}, device_id_type=pl.DeviceIdType.MESH
        )

    @pl.when(has_previous)
    def _():
        pl.semaphore_signal(barrier, inc=1, device_id={"rg": block - 1}, device_id_type=pl.DeviceIdType.MESH)

    @pl.when(has_next)
    def _():
        pl.semaphore_signal(barrier, inc=1, device_id={"rg": block + 1}, device_id_type=pl.DeviceIdType.MESH)

    pl.semaphore_wait(barrier, banks - 1 + has_previous.astype(jnp.int32) + has_next.astype(jnp.int32))

    for chunk in range(chunks):
        load(chunk).wait()

        @pl.loop(0, TILE // 16)
        def _(step):
            at = pl.ds(pl.multiple_of(chunk * TILE + step * 16, 16), 16)
            window[:, at] = stage[:, at].astype(bf16)

        if chunk < reach:

            @pl.when(has_previous)
            def _():
                rim(chunk).start()

    @pl.when(jnp.logical_not(has_next))
    def _():
        window[:, rows : rows + reach * TILE] = jnp.zeros((2, reach * TILE, first * second), bf16)
        spectra[:, rows : rows + RIM_ROWS] = jnp.zeros((banks, RIM_ROWS, first * 128), bf16)

    def shifted(index):
        whole = jnp.broadcast_to(code_ref[index], (TILE, span))
        return split(pltpu.roll(whole, 0, 1, stride=1, stride_axis=0))

    for part, (c, s) in enumerate(zip(shifted(0), shifted(1))):
        at = 2 * TILE * part
        band[at : at + TILE, :span] = c
        band[at : at + TILE, span:] = s
        band[at + TILE : at + 2 * TILE, :span] = -s
        band[at + TILE : at + 2 * TILE, span:] = c

    @pl.loop(0, chunks)
    def _(chunk):
        start = pl.multiple_of(chunk * TILE, TILE)

        @pl.when(jnp.logical_and(has_next, jnp.logical_and(chunk > 0, chunk <= reach)))
        def _():
            rim(chunk - 1).wait_recv()

        @pl.loop(0, first)
        def _(step):
            lanes = pl.ds(pl.multiple_of(step * second, second), second)
            both = jnp.concatenate([window[0, pl.ds(start, span), lanes], window[1, pl.ds(start, span), lanes]], axis=0)
            product = jnp.dot(band[...], both, preferred_element_type=f32)
            comp[step, 0] = product[:TILE] + product[2 * TILE : 3 * TILE]
            comp[step, 1] = product[TILE : 2 * TILE] + product[3 * TILE :]

        @pl.loop(0, TILE // 16)
        def _(step):
            at = pl.multiple_of(step * 16, 16)
            for lane in range(0, second, 128):
                lanes = slice(lane, lane + 128)
                values = [(comp[a, 0, pl.ds(at, 16), lanes], comp[a, 1, pl.ds(at, 16), lanes]) for a in range(first)]
                values = butterfly(values, -1, turn_pair)
                for k, (re, im) in enumerate(values):
                    c, s = twist_ref[0, k : k + 1, lanes], twist_ref[1, k : k + 1, lanes]
                    where = pl.ds(pl.multiple_of(k * TILE + at, 16), 16)
                    for base, value in ((0, re * c + im * s), (second, im * c - re * s)):
                        high, low = split(value)
                        spread_high[where, base + lane : base + lane + 128] = high
                        spread_low[where, base + lane : base + lane + 128] = low

        high = spread_high[...]
        result[...] = (
            jnp.dot(high, high_ref[...], preferred_element_type=f32)
            + jnp.dot(high, low_ref[...], preferred_element_type=f32)
            + jnp.dot(spread_low[...], high_ref[...], preferred_element_type=f32)
        )
        for k in range(first):
            for g in range(banks):
                send[g, pl.ds(start, TILE), k * 128 : (k + 1) * 128] = result[
                    k * TILE : (k + 1) * TILE, g * 128 : (g + 1) * 128
                ].astype(bf16)
        for distance in range(1, banks):
            outward(chunk, distance).start()
        spectra[bank, pl.ds(start, TILE)] = send[bank, pl.ds(start, TILE)]

    for distance in range(1, banks):
        outward(0, distance).wait_recv()

    @pl.when(has_previous)
    def _():
        edge().start()

    left = lax.broadcasted_iota(jnp.int32, (1, 128), 1) < HALF
    minus = jnp.where(left, -1.0, 1.0).astype(f32)
    quarter = jnp.where(left, 0.0, 0.25).astype(f32)

    def turn_lanes(value, c, s):
        crossed = pltpu.roll(value, HALF, 1) * minus
        if c == 0.0:
            return crossed if s > 0 else -crossed
        return value * c + crossed * s

    @pl.loop(0, chunks)
    def _(chunk):
        start = pl.multiple_of(chunk * TILE, TILE)

        @pl.when(chunk < chunks - 1)
        def _():
            for distance in range(1, banks):
                outward(chunk + 1, distance).wait_recv()

        @pl.when(jnp.logical_and(chunk == chunks - 1, has_next))
        def _():
            edge().wait_recv()

        for b in range(banks):
            steps = (
                lax.broadcasted_iota(jnp.int32, (TILE, wide), 1)
                - lax.broadcasted_iota(jnp.int32, (TILE, wide), 0)
                - offset_ref[b]
            )
            total = jnp.zeros((TILE, wide), f32)
            for t in range(taps):
                total = jnp.where(steps == t, weight_ref[b, pl.ds(start, TILE), t : t + 1], total)
            high, low = split(total)
            taps_band[b, :TILE] = high
            taps_band[b, TILE:] = low

        @pl.loop(0, first * 128 // width)
        def _(part):
            offset = pl.multiple_of(part * width, width)

            @pl.loop(0, wide // 32)
            def _(step):
                at = pl.multiple_of(step * 32, 32)
                for lane in range(0, width, 128):
                    lanes = pl.ds(pl.multiple_of(offset + lane, 128), 128)
                    values = [spectra[a, pl.ds(start + at, 32), lanes].astype(f32) for a in range(banks)]
                    for b, value in enumerate(butterfly(values, -1, turn_lanes)):
                        high, low = split(value)
                        spec_high[b, pl.ds(at, 32), lane : lane + 128] = high
                        spec_low[b, pl.ds(at, 32), lane : lane + 128] = low

            for b in range(banks):
                product = jnp.dot(taps_band[b], spec_high[b], preferred_element_type=f32)
                rest = jnp.dot(taps_band[b, :TILE], spec_low[b], preferred_element_type=f32)
                moved[b] = product[:TILE] + product[TILE:] + rest

            @pl.loop(0, TILE // 32)
            def _(step):
                at = pl.multiple_of(step * 32, 32)
                rate = rate_ref[pl.ds(start + at, 32)]
                for lane in range(0, width, 128):
                    lanes = pl.ds(pl.multiple_of(offset + lane, 128), 128)
                    values = []
                    for b in range(banks):
                        wave = cosine_turns(rate * base_ref[b : b + 1, lanes] - quarter)
                        crossed = pltpu.roll(wave, HALF, 1)
                        value = moved[b, pl.ds(at, 32), lane : lane + 128]
                        values.append(
                            value * jnp.where(left, wave, crossed)
                            + pltpu.roll(value, HALF, 1) * jnp.where(left, -crossed, wave)
                        )
                    for a, value in enumerate(butterfly(values, 1, turn_lanes)):
                        folded[a, pl.ds(start + at, 32), lanes] = value.astype(bf16)

        for distance in range(1, banks):
            backward(chunk, distance).start()
        own_back(chunk).start()

    @pl.when(has_previous)
    def _():
        for piece in range(reach):
            rim(piece).wait_send()
        edge().wait_send()

    @pl.when(has_next)
    def _():
        for piece in range(max(chunks - 1, 0), reach):
            rim(piece).wait_recv()

    @pl.loop(0, chunks)
    def _(chunk):
        for distance in range(1, banks):
            outward(chunk, distance).wait_send()
            backward(chunk, distance).wait()
        own_back(chunk).wait()


def focus_call(echo, code, twist, high, low, offsets, weights, rate, base, banks):
    first, second = twist.shape[1:]
    rows = echo.shape[1]
    chunks = rows // TILE
    span = code.shape[2]
    reach = span // TILE - 1
    lanes = first * 128
    width = min(256, lanes)
    vmem = pl.BlockSpec(memory_space=pltpu.VMEM)
    dma = pltpu.SemaphoreType.DMA
    return pl.pallas_call(
        functools.partial(focus_kernel, banks, first, second, weights.shape[2]),
        in_specs=[pl.BlockSpec(memory_space=pl.ANY), vmem, vmem, vmem, vmem, pl.BlockSpec(memory_space=pltpu.SMEM), vmem, vmem, vmem],
        out_specs=pl.BlockSpec(memory_space=pl.ANY),
        out_shape=jax.ShapeDtypeStruct((banks, rows, lanes), bf16),
        scratch_shapes=[
            pltpu.VMEM((2, rows, first * second), f32),
            pltpu.VMEM((2, rows + reach * TILE, first * second), bf16),
            pltpu.VMEM((4 * TILE, 2 * span), bf16),
            pltpu.VMEM((first, 2, TILE, second), f32),
            pltpu.VMEM((first * TILE, 2 * second), bf16),
            pltpu.VMEM((first * TILE, 2 * second), bf16),
            pltpu.VMEM((first * TILE, 2 * second), f32),
            pltpu.VMEM((banks, rows, lanes), bf16),
            pltpu.VMEM((banks, rows + RIM_ROWS, lanes), bf16),
            pltpu.VMEM((banks, 2 * TILE, TILE + RIM_ROWS), bf16),
            pltpu.VMEM((banks, TILE + RIM_ROWS, width), bf16),
            pltpu.VMEM((banks, TILE + RIM_ROWS, width), bf16),
            pltpu.VMEM((banks, TILE, width), f32),
            pltpu.VMEM((banks, rows, lanes), bf16),
            dma((chunks,)),
            dma((reach,)),
            dma((reach,)),
            dma((chunks, banks - 1)),
            dma((chunks, banks - 1)),
            dma,
            dma,
            dma((chunks, banks - 1)),
            dma((chunks, banks - 1)),
            dma((chunks,)),
        ],
        compiler_params=pltpu.CompilerParams(vmem_limit_bytes=VMEM_LIMIT, collective_id=0, has_side_effects=True),
        cost_estimate=pl.CostEstimate(flops=rows * 34_000_000, bytes_accessed=rows * 30_000, transcendentals=0),
        name="focus",
    )(echo, code, twist, high, low, offsets, weights, rate, base)


def inverse_kernel(first, second, banks, in_ref, twist_ref, high_ref, low_ref, *refs):
    out_ref, gathered, turned = refs[-3:]
    for k in range(first):
        for g in range(banks):
            gathered[k * TILE : (k + 1) * TILE, g * 128 : (g + 1) * 128] = in_ref[g, :, k * 128 : (k + 1) * 128]
    value = gathered[...]
    across = (((1,), (1,)), ((), ()))
    turned[...] = lax.dot_general(value, high_ref[...], across, preferred_element_type=f32) + lax.dot_general(
        value, low_ref[...], across, preferred_element_type=f32
    )

    @pl.loop(0, TILE // 16)
    def _(chunk):
        at = pl.multiple_of(chunk * 16, 16)
        for lane in range(0, second, 128):
            values = []
            for k in range(first):
                where = pl.ds(pl.multiple_of(k * TILE + at, 16), 16)
                re = turned[where, lane : lane + 128]
                im = turned[where, second + lane : second + lane + 128]
                c = twist_ref[0, k : k + 1, lane : lane + 128]
                s = twist_ref[1, k : k + 1, lane : lane + 128]
                values.append((re * c - im * s, im * c + re * s))
            for a, (re, im) in enumerate(butterfly(values, 1, turn_pair)):
                lanes = slice(a * second + lane, a * second + lane + 128)
                out_ref[0, pl.ds(at, 16), lanes] = re
                out_ref[1, pl.ds(at, 16), lanes] = im


def inverse_call(previous, received, twist, high, low, start, total_rows):
    banks, rows, lanes = received.shape
    first, second = twist.shape[1:]
    whole = lambda shape: pl.BlockSpec(shape, lambda s: (0,) * len(shape))
    specs = [pl.BlockSpec((banks, TILE, lanes), lambda s: (0, s, 0)), whole(twist.shape), whole(high.shape), whole(low.shape)]
    operands = [received, twist, high, low]
    aliases = {}
    if previous is not None:
        specs.append(pl.BlockSpec(memory_space=pl.ANY))
        operands.append(previous)
        aliases = {4: 0}
    return pl.pallas_call(
        functools.partial(inverse_kernel, first, second, banks),
        grid=(rows // TILE,),
        in_specs=specs,
        out_specs=pl.BlockSpec((2, TILE, first * second), lambda s: (0, start // TILE + s, 0)),
        out_shape=jax.ShapeDtypeStruct((2, total_rows, first * second), f32),
        scratch_shapes=[
            pltpu.VMEM((first * TILE, 2 * second), bf16),
            pltpu.VMEM((first * TILE, 2 * second), f32),
        ],
        input_output_aliases=aliases,
        compiler_params=pltpu.CompilerParams(vmem_limit_bytes=VMEM_LIMIT),
        cost_estimate=pl.CostEstimate(flops=rows * 10_000_000, bytes_accessed=rows * 30_000, transcendentals=0),
        name="inverse",
    )(*operands)


def tables(banks, first, second):
    pulses = banks * first * second
    inner = np.arange(second)
    highs, lows, twists = [], [], []
    for bank in range(banks):
        steps = banks * inner + bank
        angle = 2.0 * np.pi * ((steps[:, None] * inner[None, :]) % (banks * second)) / (banks * second)
        c, s = np.cos(angle), np.sin(angle)
        re_out = np.concatenate([c, s], axis=0).reshape(2 * second, banks, HALF)
        im_out = np.concatenate([-s, c], axis=0).reshape(2 * second, banks, HALF)
        table = np.stack([re_out, im_out], axis=2).reshape(2 * second, 2 * second)
        high = table.astype(ml_dtypes.bfloat16)
        highs.append(high)
        lows.append((table - high.astype(np.float64)).astype(ml_dtypes.bfloat16))
        angle = 2.0 * np.pi * ((np.arange(first)[:, None] * steps[None, :]) % pulses) / pulses
        twists.append(np.stack([np.cos(angle), np.sin(angle)]).astype(np.float32))
    return np.stack(highs), np.stack(lows), np.stack(twists)


def local(echo_planes, pulse_phase, band_offsets, band_weights, azimuth_rate):
    banks = lax.axis_size("az")
    bank = lax.axis_index("az")
    row_count, pulse_local = echo_planes.shape[1:]
    pulse_count = pulse_local * banks
    second = HALF * banks
    first = pulse_local // second
    code_length = pulse_phase.shape[0]
    reach = -(-code_length // TILE)
    highs, lows, twists = tables(banks, first, second)
    pick = lambda stack: lax.dynamic_index_in_dim(jnp.asarray(stack), bank, 0, keepdims=False)
    high, low, twist = pick(highs), pick(lows), pick(twists)
    span = (reach + 1) * TILE
    norm_scale = 1.0 / math.sqrt(code_length)
    code = jnp.stack([jnp.cos(pulse_phase), jnp.sin(pulse_phase)]) * norm_scale
    code = jnp.pad(code, ((0, 0), (0, span - code_length)))[:, None, :]

    offsets = band_offsets[:, 0, 0]
    weights = band_weights[:, 0].transpose(0, 2, 1)
    rate = jnp.broadcast_to(azimuth_rate[:, None], (row_count, 128))
    lane = jnp.arange(first * 128, dtype=jnp.int32)
    bins = bank * (HALF * first) + first * (lane % HALF) + lane // 128
    bins = bins[None, :] + pulse_local * jnp.arange(banks, dtype=jnp.int32)[:, None]
    centered = jnp.where(bins < pulse_count // 2, bins, bins - pulse_count)
    frequency = centered.astype(f32) / pulse_count
    base = 0.5 * frequency * frequency

    received = focus_call(echo_planes, code, twist, high, low, offsets, weights, rate, base, banks)
    return inverse_call(None, received, twist * (1.0 / pulse_count), high, low, 0, row_count)


def solution(mesh):
    in_specs = (P(None, "rg", "az"), P(), P(None, "az", "rg"), P(None, "az", None, "rg"), P("rg"))
    out_specs = P(None, "rg", "az")
    return jax.shard_map(local, mesh=mesh, in_specs=in_specs, out_specs=out_specs, check_vma=False)
```

```python
import functools
import math

import jax
import jax.numpy as jnp
import ml_dtypes
import numpy as np
from jax import lax
from jax.experimental import pallas as pl
from jax.experimental.pallas import tpu as pltpu
from jax.sharding import PartitionSpec as P

RIM_ROWS = 64
TILE = 128
HALF = 64
VMEM_LIMIT = 56 * 1024 * 1024
bf16 = jnp.bfloat16
f32 = jnp.float32


def butterfly(values, sign, turn):
    count = len(values)
    if count == 1:
        return values
    even = butterfly(values[0::2], sign, turn)
    odd = butterfly(values[1::2], sign, turn)
    lower, upper = [], []
    for k in range(count // 2):
        if k == 0:
            turned = odd[k]
        elif 4 * k == count:
            turned = turn(odd[k], 0.0, float(sign))
        else:
            angle = sign * 2.0 * math.pi * k / count
            turned = turn(odd[k], math.cos(angle), math.sin(angle))
        lower.append(jax.tree.map(lambda x, y: x + y, even[k], turned))
        upper.append(jax.tree.map(lambda x, y: x - y, even[k], turned))
    return lower + upper


def turn_pair(value, c, s):
    re, im = value
    if c == 0.0:
        return (-im, re) if s > 0 else (im, -re)
    return (re * c - im * s, im * c + re * s)


def split(value):
    high = value.astype(bf16)
    return high, (value - high.astype(f32)).astype(bf16)


SINE = [(-1) ** n * (2.0 * math.pi) ** (2 * n + 1) / math.factorial(2 * n + 1) for n in range(6)]


def cosine_turns(turns):
    rest = turns - jnp.round(turns)
    u = 0.25 - jnp.abs(rest)
    z = u * u
    total = jnp.full_like(z, SINE[-1])
    for factor in reversed(SINE[:-1]):
        total = total * z + factor
    return total * u


def focus_kernel(
    banks, first, second, taps, echo_ref, phase_ref, twist_all, high_all, low_all, offset_ref, weight_ref, rate_all, out_ref,
    stage, window, band, comp, spread_high, spread_low, result, send, spectra, taps_band, spec_high, spec_low, moved, folded,
    high_ref, low_ref, rate_ref, base_ref, load_sem, table_sem, rim_send, rim_recv, out_send, out_recv, edge_send, edge_recv, back_send, back_recv, own_sem,
):
    bank, block = lax.axis_index("az"), lax.axis_index("rg")
    block_count = lax.axis_size("rg")
    rows = echo_ref.shape[1]
    chunks = rows // TILE
    code_length = phase_ref.shape[1]
    reach = -(-code_length // TILE)
    span = (reach + 1) * TILE
    twist_ref = twist_all.at[bank]
    width = min(256, first * 128)
    wide = TILE + RIM_ROWS
    has_next = block < block_count - 1
    has_previous = block > 0

    def load(chunk):
        at = slice(chunk * TILE, (chunk + 1) * TILE)
        return pltpu.make_async_copy(echo_ref.at[:, at], stage.at[:, at], load_sem.at[chunk])

    def rim(piece):
        return pltpu.make_async_remote_copy(
            src_ref=window.at[:, pl.ds(piece * TILE, TILE)],
            dst_ref=window.at[:, pl.ds(rows + piece * TILE, TILE)],
            send_sem=rim_send.at[piece],
            recv_sem=rim_recv.at[piece],
            device_id={"rg": lax.rem(block + block_count - 1, block_count)},
            device_id_type=pl.DeviceIdType.MESH,
        )

    def edge():
        return pltpu.make_async_remote_copy(
            src_ref=spectra.at[:, pl.ds(0, RIM_ROWS)],
            dst_ref=spectra.at[:, pl.ds(rows, RIM_ROWS)],
            send_sem=edge_send,
            recv_sem=edge_recv,
            device_id={"rg": lax.rem(block + block_count - 1, block_count)},
            device_id_type=pl.DeviceIdType.MESH,
        )

    def exchange(source, target, send_sem, recv_sem, chunk, distance):
        peer = lax.rem(bank + distance, banks)
        return pltpu.make_async_remote_copy(
            src_ref=source.at[peer, pl.ds(pl.multiple_of(chunk * TILE, TILE), TILE)],
            dst_ref=target.at[bank, pl.ds(pl.multiple_of(chunk * TILE, TILE), TILE)],
            send_sem=send_sem.at[chunk, distance - 1],
            recv_sem=recv_sem.at[chunk, distance - 1],
            device_id={"az": peer},
            device_id_type=pl.DeviceIdType.MESH,
        )

    outward = functools.partial(exchange, send, spectra, out_send, out_recv)
    backward = functools.partial(exchange, folded, out_ref, back_send, back_recv)

    def own_back(chunk):
        at = pl.ds(pl.multiple_of(chunk * TILE, TILE), TILE)
        return pltpu.make_async_copy(folded.at[bank, at], out_ref.at[bank, at], own_sem.at[chunk])

    for chunk in range(chunks):
        load(chunk).start()
    table_copies = [
        pltpu.make_async_copy(source.at[bank], target, table_sem.at[index])
        for index, (source, target) in enumerate(((high_all, high_ref), (low_all, low_ref)))
    ]
    for copy in table_copies:
        copy.start()

    barrier = pltpu.get_barrier_semaphore()
    for distance in range(1, banks):
        pl.semaphore_signal(
            barrier, inc=1, device_id={"az": lax.rem(bank + distance, banks)}, device_id_type=pl.DeviceIdType.MESH
        )

    @pl.when(has_previous)
    def _():
        pl.semaphore_signal(barrier, inc=1, device_id={"rg": block - 1}, device_id_type=pl.DeviceIdType.MESH)

    @pl.when(has_next)
    def _():
        pl.semaphore_signal(barrier, inc=1, device_id={"rg": block + 1}, device_id_type=pl.DeviceIdType.MESH)

    def shifted(index):
        row = (jnp.cos, jnp.sin)[index](phase_ref[...]) * (1.0 / math.sqrt(code_length))
        row = jnp.concatenate([row, jnp.zeros((1, span - code_length), f32)], axis=1)
        whole = jnp.broadcast_to(row, (TILE, span))
        return split(pltpu.roll(whole, 0, 1, stride=1, stride_axis=0))

    for part, (c, s) in enumerate(zip(shifted(0), shifted(1))):
        at = 2 * TILE * part
        band[at : at + TILE, :span] = c
        band[at : at + TILE, span:] = s
        band[at + TILE : at + 2 * TILE, :span] = -s
        band[at + TILE : at + 2 * TILE, span:] = c

    lane_id = lax.broadcasted_iota(jnp.int32, (1, 128), 1)
    pulse_local, pulse_count = first * second, banks * first * second
    for k in range(first):
        for b in range(banks):
            bins = bank * (HALF * first) + first * (lane_id % HALF) + (k + pulse_local * b)
            centered = jnp.where(bins < pulse_count // 2, bins, bins - pulse_count)
            frequency = centered.astype(f32) * (1.0 / pulse_count)
            base_ref[b : b + 1, k * 128 : (k + 1) * 128] = 0.5 * frequency * frequency

    pl.semaphore_wait(barrier, banks - 1 + has_previous.astype(jnp.int32) + has_next.astype(jnp.int32))

    for chunk in range(chunks):
        load(chunk).wait()

        @pl.loop(0, TILE // 16)
        def _(step):
            at = pl.ds(pl.multiple_of(chunk * TILE + step * 16, 16), 16)
            window[:, at] = stage[:, at].astype(bf16)

        if chunk < reach:

            @pl.when(has_previous)
            def _():
                rim(chunk).start()

    @pl.when(jnp.logical_not(has_next))
    def _():
        window[:, rows : rows + reach * TILE] = jnp.zeros((2, reach * TILE, first * second), bf16)
        spectra[:, rows : rows + RIM_ROWS] = jnp.zeros((banks, RIM_ROWS, first * 128), bf16)

    for copy in table_copies:
        copy.wait()

    @pl.loop(0, chunks)
    def _(chunk):
        start = pl.multiple_of(chunk * TILE, TILE)

        @pl.when(jnp.logical_and(has_next, jnp.logical_and(chunk > 0, chunk <= reach)))
        def _():
            rim(chunk - 1).wait_recv()

        @pl.loop(0, first)
        def _(step):
            lanes = pl.ds(pl.multiple_of(step * second, second), second)
            both = jnp.concatenate([window[0, pl.ds(start, span), lanes], window[1, pl.ds(start, span), lanes]], axis=0)
            product = jnp.dot(band[...], both, preferred_element_type=f32)
            comp[step, 0] = product[:TILE] + product[2 * TILE : 3 * TILE]
            comp[step, 1] = product[TILE : 2 * TILE] + product[3 * TILE :]

        @pl.loop(0, TILE // 16)
        def _(step):
            at = pl.multiple_of(step * 16, 16)
            for lane in range(0, second, 128):
                lanes = slice(lane, lane + 128)
                values = [(comp[a, 0, pl.ds(at, 16), lanes], comp[a, 1, pl.ds(at, 16), lanes]) for a in range(first)]
                values = butterfly(values, -1, turn_pair)
                for k, (re, im) in enumerate(values):
                    c, s = twist_ref[0, k : k + 1, lanes], twist_ref[1, k : k + 1, lanes]
                    where = pl.ds(pl.multiple_of(k * TILE + at, 16), 16)
                    for base, value in ((0, re * c + im * s), (second, im * c - re * s)):
                        high, low = split(value)
                        spread_high[where, base + lane : base + lane + 128] = high
                        spread_low[where, base + lane : base + lane + 128] = low

        high = spread_high[...]
        result[...] = (
            jnp.dot(high, high_ref[...], preferred_element_type=f32)
            + jnp.dot(high, low_ref[...], preferred_element_type=f32)
            + jnp.dot(spread_low[...], high_ref[...], preferred_element_type=f32)
        )
        for k in range(first):
            for g in range(banks):
                send[g, pl.ds(start, TILE), k * 128 : (k + 1) * 128] = result[
                    k * TILE : (k + 1) * TILE, g * 128 : (g + 1) * 128
                ].astype(bf16)
        for distance in range(1, banks):
            outward(chunk, distance).start()
        spectra[bank, pl.ds(start, TILE)] = send[bank, pl.ds(start, TILE)]

    for distance in range(1, banks):
        outward(0, distance).wait_recv()

    @pl.when(has_previous)
    def _():
        edge().start()

    left = lax.broadcasted_iota(jnp.int32, (1, 128), 1) < HALF
    minus = jnp.where(left, -1.0, 1.0).astype(f32)
    quarter = jnp.where(left, 0.0, 0.25).astype(f32)

    def turn_lanes(value, c, s):
        crossed = pltpu.roll(value, HALF, 1) * minus
        if c == 0.0:
            return crossed if s > 0 else -crossed
        return value * c + crossed * s

    @pl.loop(0, chunks)
    def _(chunk):
        start = pl.multiple_of(chunk * TILE, TILE)

        @pl.when(chunk < chunks - 1)
        def _():
            for distance in range(1, banks):
                outward(chunk + 1, distance).wait_recv()

        @pl.when(jnp.logical_and(chunk == chunks - 1, has_next))
        def _():
            edge().wait_recv()

        rate_ref[...] = jnp.broadcast_to(rate_all[:, pl.ds(start, TILE)], (128, TILE)).T
        for b in range(banks):
            turned = weight_ref[b, 0, :, pl.ds(start, TILE)].T
            steps = (
                lax.broadcasted_iota(jnp.int32, (TILE, wide), 1)
                - lax.broadcasted_iota(jnp.int32, (TILE, wide), 0)
                - offset_ref[b]
            )
            total = jnp.zeros((TILE, wide), f32)
            for t in range(taps):
                total = jnp.where(steps == t, turned[:, t : t + 1], total)
            high, low = split(total)
            taps_band[b, :TILE] = high
            taps_band[b, TILE:] = low

        @pl.loop(0, first * 128 // width)
        def _(part):
            offset = pl.multiple_of(part * width, width)

            @pl.loop(0, wide // 32)
            def _(step):
                at = pl.multiple_of(step * 32, 32)
                for lane in range(0, width, 128):
                    lanes = pl.ds(pl.multiple_of(offset + lane, 128), 128)
                    values = [spectra[a, pl.ds(start + at, 32), lanes].astype(f32) for a in range(banks)]
                    for b, value in enumerate(butterfly(values, -1, turn_lanes)):
                        high, low = split(value)
                        spec_high[b, pl.ds(at, 32), lane : lane + 128] = high
                        spec_low[b, pl.ds(at, 32), lane : lane + 128] = low

            for b in range(banks):
                product = jnp.dot(taps_band[b], spec_high[b], preferred_element_type=f32)
                rest = jnp.dot(taps_band[b, :TILE], spec_low[b], preferred_element_type=f32)
                moved[b] = product[:TILE] + product[TILE:] + rest

            @pl.loop(0, TILE // 32)
            def _(step):
                at = pl.multiple_of(step * 32, 32)
                rate = rate_ref[pl.ds(at, 32)]
                for lane in range(0, width, 128):
                    lanes = pl.ds(pl.multiple_of(offset + lane, 128), 128)
                    values = []
                    for b in range(banks):
                        wave = cosine_turns(rate * base_ref[b : b + 1, lanes] - quarter)
                        crossed = pltpu.roll(wave, HALF, 1)
                        value = moved[b, pl.ds(at, 32), lane : lane + 128]
                        values.append(
                            value * jnp.where(left, wave, crossed)
                            + pltpu.roll(value, HALF, 1) * jnp.where(left, -crossed, wave)
                        )
                    for a, value in enumerate(butterfly(values, 1, turn_lanes)):
                        folded[a, pl.ds(start + at, 32), lanes] = value.astype(bf16)

        for distance in range(1, banks):
            backward(chunk, distance).start()
        own_back(chunk).start()

    @pl.when(has_previous)
    def _():
        for piece in range(reach):
            rim(piece).wait_send()
        edge().wait_send()

    @pl.when(has_next)
    def _():
        for piece in range(max(chunks - 1, 0), reach):
            rim(piece).wait_recv()

    @pl.loop(0, chunks)
    def _(chunk):
        for distance in range(1, banks):
            outward(chunk, distance).wait_send()
            backward(chunk, distance).wait()
        own_back(chunk).wait()


def focus_call(echo, phase, twist, high, low, offsets, weights, rate, banks):
    first, second = twist.shape[2:]
    rows = echo.shape[1]
    chunks = rows // TILE
    reach = -(-phase.shape[1] // TILE)
    span = (reach + 1) * TILE
    lanes = first * 128
    width = min(256, lanes)
    vmem = pl.BlockSpec(memory_space=pltpu.VMEM)
    anywhere = pl.BlockSpec(memory_space=pl.ANY)
    dma = pltpu.SemaphoreType.DMA
    return pl.pallas_call(
        functools.partial(focus_kernel, banks, first, second, weights.shape[2]),
        in_specs=[anywhere, vmem, vmem, anywhere, anywhere, pl.BlockSpec(memory_space=pltpu.SMEM), vmem, vmem],
        out_specs=pl.BlockSpec(memory_space=pl.ANY),
        out_shape=jax.ShapeDtypeStruct((banks, rows, lanes), bf16),
        scratch_shapes=[
            pltpu.VMEM((2, rows, first * second), f32),
            pltpu.VMEM((2, rows + reach * TILE, first * second), bf16),
            pltpu.VMEM((4 * TILE, 2 * span), bf16),
            pltpu.VMEM((first, 2, TILE, second), f32),
            pltpu.VMEM((first * TILE, 2 * second), bf16),
            pltpu.VMEM((first * TILE, 2 * second), bf16),
            pltpu.VMEM((first * TILE, 2 * second), f32),
            pltpu.VMEM((banks, rows, lanes), bf16),
            pltpu.VMEM((banks, rows + RIM_ROWS, lanes), bf16),
            pltpu.VMEM((banks, 2 * TILE, TILE + RIM_ROWS), bf16),
            pltpu.VMEM((banks, TILE + RIM_ROWS, width), bf16),
            pltpu.VMEM((banks, TILE + RIM_ROWS, width), bf16),
            pltpu.VMEM((banks, TILE, width), f32),
            pltpu.VMEM((banks, rows, lanes), bf16),
            pltpu.VMEM((2 * second, 2 * second), bf16),
            pltpu.VMEM((2 * second, 2 * second), bf16),
            pltpu.VMEM((TILE, 128), f32),
            pltpu.VMEM((banks, lanes), f32),
            dma((chunks,)),
            dma((2,)),
            dma((reach,)),
            dma((reach,)),
            dma((chunks, banks - 1)),
            dma((chunks, banks - 1)),
            dma,
            dma,
            dma((chunks, banks - 1)),
            dma((chunks, banks - 1)),
            dma((chunks,)),
        ],
        compiler_params=pltpu.CompilerParams(vmem_limit_bytes=VMEM_LIMIT, collective_id=0, has_side_effects=True),
        cost_estimate=pl.CostEstimate(flops=rows * 34_000_000, bytes_accessed=rows * 30_000, transcendentals=0),
        name="focus",
    )(echo, phase, twist, high, low, offsets, weights, rate)


def inverse_kernel(first, second, banks, in_ref, twist_all, high_all, low_all, out_ref, gathered, turned, high_ref, low_ref, table_sem):
    bank = lax.axis_index("az")
    twist_ref = twist_all.at[bank]
    scale = 1.0 / (banks * first * second)

    @pl.when(pl.program_id(0) == 0)
    def _():
        copies = [
            pltpu.make_async_copy(source.at[bank], target, table_sem.at[index])
            for index, (source, target) in enumerate(((high_all, high_ref), (low_all, low_ref)))
        ]
        for copy in copies:
            copy.start()
        for copy in copies:
            copy.wait()

    for k in range(first):
        for g in range(banks):
            gathered[k * TILE : (k + 1) * TILE, g * 128 : (g + 1) * 128] = in_ref[g, :, k * 128 : (k + 1) * 128]
    value = gathered[...]
    across = (((1,), (1,)), ((), ()))
    turned[...] = lax.dot_general(value, high_ref[...], across, preferred_element_type=f32) + lax.dot_general(
        value, low_ref[...], across, preferred_element_type=f32
    )

    @pl.loop(0, TILE // 16)
    def _(chunk):
        at = pl.multiple_of(chunk * 16, 16)
        for lane in range(0, second, 128):
            values = []
            for k in range(first):
                where = pl.ds(pl.multiple_of(k * TILE + at, 16), 16)
                re = turned[where, lane : lane + 128]
                im = turned[where, second + lane : second + lane + 128]
                c = twist_ref[0, k : k + 1, lane : lane + 128] * scale
                s = twist_ref[1, k : k + 1, lane : lane + 128] * scale
                values.append((re * c - im * s, im * c + re * s))
            for a, (re, im) in enumerate(butterfly(values, 1, turn_pair)):
                lanes = slice(a * second + lane, a * second + lane + 128)
                out_ref[0, pl.ds(at, 16), lanes] = re
                out_ref[1, pl.ds(at, 16), lanes] = im


def inverse_call(received, twist, high, low):
    banks, rows, lanes = received.shape
    first, second = twist.shape[2:]
    anywhere = pl.BlockSpec(memory_space=pl.ANY)
    specs = [
        pl.BlockSpec((banks, TILE, lanes), lambda s: (0, s, 0)),
        pl.BlockSpec(twist.shape, lambda s: (0, 0, 0, 0)),
        anywhere,
        anywhere,
    ]
    return pl.pallas_call(
        functools.partial(inverse_kernel, first, second, banks),
        grid=(rows // TILE,),
        in_specs=specs,
        out_specs=pl.BlockSpec((2, TILE, first * second), lambda s: (0, s, 0)),
        out_shape=jax.ShapeDtypeStruct((2, rows, first * second), f32),
        scratch_shapes=[
            pltpu.VMEM((first * TILE, 2 * second), bf16),
            pltpu.VMEM((first * TILE, 2 * second), f32),
            pltpu.VMEM((2 * second, 2 * second), bf16),
            pltpu.VMEM((2 * second, 2 * second), bf16),
            pltpu.SemaphoreType.DMA((2,)),
        ],
        compiler_params=pltpu.CompilerParams(vmem_limit_bytes=VMEM_LIMIT),
        cost_estimate=pl.CostEstimate(flops=rows * 10_000_000, bytes_accessed=rows * 30_000, transcendentals=0),
        name="inverse",
    )(received, twist, high, low)


def tables(banks, first, second):
    pulses = banks * first * second
    inner = np.arange(second)
    highs, lows, twists = [], [], []
    for bank in range(banks):
        steps = banks * inner + bank
        angle = 2.0 * np.pi * ((steps[:, None] * inner[None, :]) % (banks * second)) / (banks * second)
        c, s = np.cos(angle), np.sin(angle)
        re_out = np.concatenate([c, s], axis=0).reshape(2 * second, banks, HALF)
        im_out = np.concatenate([-s, c], axis=0).reshape(2 * second, banks, HALF)
        table = np.stack([re_out, im_out], axis=2).reshape(2 * second, 2 * second)
        high = table.astype(ml_dtypes.bfloat16)
        highs.append(high)
        lows.append((table - high.astype(np.float64)).astype(ml_dtypes.bfloat16))
        angle = 2.0 * np.pi * ((np.arange(first)[:, None] * steps[None, :]) % pulses) / pulses
        twists.append(np.stack([np.cos(angle), np.sin(angle)]).astype(np.float32))
    return np.stack(highs), np.stack(lows), np.stack(twists)


def local(echo_planes, pulse_phase, band_offsets, band_weights, azimuth_rate):
    banks = lax.axis_size("az")
    second = HALF * banks
    high, low, twist = (jnp.asarray(table) for table in tables(banks, echo_planes.shape[2] // second, second))
    received = focus_call(
        echo_planes, pulse_phase[None], twist, high, low, band_offsets[:, 0, 0], band_weights, azimuth_rate[None], banks
    )
    return inverse_call(received, twist, high, low)


def solution(mesh):
    in_specs = (P(None, "rg", "az"), P(), P(None, "az", "rg"), P(None, "az", None, "rg"), P("rg"))
    out_specs = P(None, "rg", "az")
    return jax.shard_map(local, mesh=mesh, in_specs=in_specs, out_specs=out_specs, check_vma=False)
```
